32 devices in a mesh: dp: 8 (over z, core), expert: 4 (over y, x).
Axes of the slice: x: 2, y: 2, z: 4, core: 2. Of those that a mesh axis runs over, the one named last changes fastest.
Arguments:
- tokens: bfloat16 [1280, 4096], P('expert', 'dp'), may hold values from -6 to 6
- out_grad: bfloat16 [1280, 4096], P('expert', 'dp'), may hold values from -0.29882812 to 0.29882812
- slot_tokens: int32 [1, 40], replicated, may hold values from 0 to 1279, as said below
- slot_gate: float32 [1, 40], replicated, may hold values from 0.1 to 1
- w_gate: bfloat16 [4, 4096, 2048], P('expert', 'dp'), may hold values from -0.09375 to 0.09375
- w_up: bfloat16 [4, 4096, 2048], P('expert', 'dp'), may hold values from -0.09375 to 0.09375
- w_down: bfloat16 [4, 2048, 4096], P('expert', None, 'dp'), may hold values from -0.0625 to 0.0625
Outputs:
- grad_tokens: bfloat16 [1280, 4096], P('expert', 'dp')
- grad_w_gate: bfloat16 [4, 4096, 2048], P('expert', 'dp')
- grad_w_up: bfloat16 [4, 4096, 2048], P('expert', 'dp')
- grad_w_down: bfloat16 [4, 2048, 4096], P('expert', None, 'dp')
- grad_gates: float32 [4, 10], P('expert')
The draws below stay inside these ranges and needn't reach their ends.
Inputs may be any that keep to these rules, and one draw needn't show every extreme that they name: `slot_tokens`: row e lists 40 distinct token numbers, ordered by their owner t // 320 ascending. At most 20 of a row come from the 320 tokens of one owner, and in every row exactly 20 come from one owner.
All inputs are finite; a program needn't handle non-finite values.
Results may differ from the reference program's by a relative error of at most 0.0057.
Values may be sent and summed in bfloat16 or wider, within the bound.
A program may use at most 64 MiB of HBM per device.

```python
from functools import partial
import jax
import jax.numpy as jnp
from jax import lax

D = 4096
FF_WIN = 8192
GROUP = 4
TOK_DEV = 320
TOKENS = 1280
FLIGHT = 1
FF_Q = 2048
CAP = 40
MOST = 20
N_EXPERT = 4


def draw_slot_tokens(key, part):
    key_hot = jax.random.fold_in(key, 11)
    key_pick = jax.random.fold_in(key, 12)
    key_order = jax.random.fold_in(key, 13)
    hot_owner = jax.random.randint(key_hot, (FLIGHT,), 0, N_EXPERT, dtype=jnp.int32)
    spare_slots = MOST - 1
    candidates = (N_EXPERT - 1) * spare_slots
    pick_keys = jax.random.split(key_pick, FLIGHT)
    orders = jax.vmap(partial(jax.random.permutation, x=candidates))(pick_keys)
    chosen = orders[:, :CAP - MOST].astype(jnp.int32)
    offset = chosen // spare_slots
    owner_of = (hot_owner[:, None] + 1 + offset) % N_EXPERT
    owner_range = jnp.arange(N_EXPERT, dtype=jnp.int32)
    counts = jnp.sum((owner_of[:, :, None] == owner_range[None, None, :]).astype(jnp.int32), axis=1)
    counts = counts + MOST * (owner_range[None, :] == hot_owner[:, None]).astype(jnp.int32)
    bucket_ends = jnp.cumsum(counts, axis=1)
    bucket_starts = bucket_ends - counts
    slot_range = jnp.arange(CAP, dtype=jnp.int32)
    owner_slot = jnp.sum((bucket_ends[:, None, :] <= slot_range[None, :, None]).astype(jnp.int32), axis=2)
    start_slot = jnp.take_along_axis(bucket_starts, owner_slot, axis=1)
    rank_slot = slot_range[None, :] - start_slot
    order_keys = jax.random.split(key_order, FLIGHT * N_EXPERT)
    local_orders = jax.vmap(partial(jax.random.permutation, x=TOK_DEV))(order_keys)
    local_orders = local_orders.reshape(FLIGHT, N_EXPERT, TOK_DEV).astype(jnp.int32)
    expert_range = jnp.arange(FLIGHT, dtype=jnp.int32)[:, None]
    local_token = local_orders[expert_range, owner_slot, rank_slot]
    return (owner_slot * TOK_DEV + local_token).astype(jnp.int32)


def block_scale(key, extent, pieces, least, top_value):
    factor_of, own = 1.0, jax.random.fold_in(key, 6)
    for dim, shards_of in pieces:
        heights = jnp.exp(jax.random.uniform(jax.random.fold_in(own, dim), (shards_of,), jnp.float32, least / len(pieces), top_value / len(pieces)))
        factor_of = factor_of * jnp.repeat(heights, extent[dim] // shards_of).reshape([-1 if axis == dim else 1 for axis in range(len(extent))])
    return factor_of


def gaussian(own_key, dims, width, bound, shards=(), kind=jnp.bfloat16):
    gain = block_scale(own_key, dims, shards, -0.22, 0.18) if shards else 1.0
    result = jax.random.normal(own_key, dims, jnp.float32) * width * gain
    return jnp.minimum(jnp.maximum(result, -bound), bound).astype(kind)


def setup_inputs(seed: int = 0) -> dict:
    arg_keys = jax.random.split(jax.random.key(seed), 8)
    tokens = gaussian(arg_keys[0], (TOKENS, D), 1.0, 6.0, ((0, 4), (1, 8)))
    out_grad = gaussian(arg_keys[1], (TOKENS, D), 0.05, 0.29882812, ((0, 4), (1, 8)))
    slot_tokens = draw_slot_tokens(jax.random.fold_in(arg_keys[7], 71), 0)
    slot_gate = jnp.clip(jax.random.uniform(arg_keys[3], (FLIGHT, CAP), jnp.float32, 0.1, 1.0), 0.1, 1.0)
    w_gate = gaussian(arg_keys[4], (FLIGHT * GROUP, D, FF_Q), D ** -0.5, 0.09375, ((0, 4), (1, 8)))
    w_up = gaussian(arg_keys[5], (FLIGHT * GROUP, D, FF_Q), D ** -0.5, 0.09375, ((0, 4), (1, 8)))
    w_down = gaussian(arg_keys[6], (FLIGHT * GROUP, FF_Q, D), FF_WIN ** -0.5, 0.0625, ((0, 4), (2, 8)))
    return dict(tokens=tokens, out_grad=out_grad, slot_tokens=slot_tokens, slot_gate=slot_gate, w_gate=w_gate, w_up=w_up, w_down=w_down)


def reference(tokens, out_grad, slot_tokens, slot_gate, w_gate, w_up, w_down):
    gate_parts_all = w_gate.reshape(FLIGHT, GROUP, D, FF_Q)
    up_parts_all = w_up.reshape(FLIGHT, GROUP, D, FF_Q)
    down_parts_all = w_down.reshape(FLIGHT, GROUP * FF_Q, D)

    def one_expert(operands):
        chosen, gates, gate_parts, up_parts, down_matrix = operands
        gate_matrix = jnp.transpose(gate_parts, (1, 0, 2)).reshape(D, FF_WIN)
        up_matrix = jnp.transpose(up_parts, (1, 0, 2)).reshape(D, FF_WIN)
        slot_inputs = tokens[chosen]
        slot_grads = out_grad[chosen]
        pre_gate = jnp.dot(slot_inputs, gate_matrix, preferred_element_type=jnp.float32)
        pre_up = jnp.dot(slot_inputs, up_matrix, preferred_element_type=jnp.float32)
        sigmoid_gate = jax.nn.sigmoid(pre_gate)
        hidden = (pre_gate * sigmoid_gate * pre_up).astype(jnp.bfloat16)
        expert_out = jnp.dot(hidden, down_matrix, preferred_element_type=jnp.float32)
        gate_grad = jnp.sum(slot_grads.astype(jnp.float32) * expert_out, axis=1)
        scaled = (gates[:, None] * slot_grads.astype(jnp.float32)).astype(jnp.bfloat16)
        down_grad = jnp.dot(hidden.T, scaled, preferred_element_type=jnp.float32).astype(jnp.bfloat16)
        hidden_grad = jnp.dot(scaled, down_matrix.T, preferred_element_type=jnp.float32)
        gate_side = (hidden_grad * pre_up * sigmoid_gate * (1.0 + pre_gate * (1.0 - sigmoid_gate))).astype(jnp.bfloat16)
        up_side = (hidden_grad * pre_gate * sigmoid_gate).astype(jnp.bfloat16)
        gate_w_grad = jnp.dot(slot_inputs.T, gate_side, preferred_element_type=jnp.float32).astype(jnp.bfloat16)
        up_w_grad = jnp.dot(slot_inputs.T, up_side, preferred_element_type=jnp.float32).astype(jnp.bfloat16)
        input_grad = jnp.dot(gate_side, gate_matrix.T, preferred_element_type=jnp.float32)
        input_grad = input_grad + jnp.dot(up_side, up_matrix.T, preferred_element_type=jnp.float32)
        gate_w_grad = jnp.transpose(gate_w_grad.reshape(D, GROUP, FF_Q), (1, 0, 2))
        up_w_grad = jnp.transpose(up_w_grad.reshape(D, GROUP, FF_Q), (1, 0, 2))
        return gate_w_grad, up_w_grad, down_grad.reshape(GROUP, FF_Q, D), input_grad, gate_grad

    results = lax.map(one_expert, (slot_tokens, slot_gate, gate_parts_all, up_parts_all, down_parts_all))
    gate_w_grads, up_w_grads, down_grads, input_grads, gate_grads = results
    summed = jnp.zeros((TOKENS, D), jnp.float32).at[slot_tokens.reshape(-1)].add(input_grads.reshape(FLIGHT * CAP, D))
    grad_tokens = summed.astype(jnp.bfloat16)
    grad_w_gate = gate_w_grads.reshape(FLIGHT * GROUP, D, FF_Q)
    grad_w_up = up_w_grads.reshape(FLIGHT * GROUP, D, FF_Q)
    grad_w_down = down_grads.reshape(FLIGHT * GROUP, FF_Q, D)
    grad_gates = gate_grads.reshape(FLIGHT * GROUP, CAP // GROUP)
    return (grad_tokens, grad_w_gate, grad_w_up, grad_w_down, grad_gates)
```

```python
import functools

import jax
import jax.numpy as jnp
from jax import lax
from jax.experimental import pallas as pl
from jax.experimental.pallas import tpu as pltpu
from jax.sharding import PartitionSpec as P

GROUP = 4
MESH = pl.DeviceIdType.MESH
BF16 = jnp.bfloat16
F32 = jnp.float32


def ceil_to(value, step):
    return -(-value // step) * step


def mm(left, right, left_dim, right_dim):
    return lax.dot_general(
        left, right, (((left_dim,), (right_dim,)), ((), ())), preferred_element_type=F32
    )


def iota(shape, dim):
    return lax.broadcasted_iota(jnp.int32, shape, dim)


def count_below(row, bound):
    return jnp.sum(jnp.where(row < bound, 1.0, 0.0), axis=1, keepdims=True).astype(jnp.int32)


def rank_mask(row, low, high, rows, columns_dim):
    capacity = row.shape[1]
    start, end = count_below(row, low), count_below(row, high)
    shape = (rows, capacity) if columns_dim == 1 else (capacity, rows)
    slot, rank = iota(shape, columns_dim), iota(shape, 1 - columns_dim)
    return (slot == rank + start) & (slot < end)


def local_index(row, low, high, rows):
    mask = rank_mask(row, low, high, rows, 1)
    shifted = (row + (1 - low)).astype(F32)
    picked = jnp.sum(jnp.where(mask, shifted, 0.0), axis=1, keepdims=True)
    return picked.astype(jnp.int32) - 1


def row_to_column(row):
    size = row.shape[1]
    eye = iota((size, size), 0) == iota((size, size), 1)
    return jnp.sum(jnp.where(eye, row, 0.0), axis=1, keepdims=True)


def split_two(value):
    high = value.astype(BF16).astype(F32)
    return [high, value - high]


def pick_row(table, index):
    if table.shape[0] == 1:
        return table
    return jnp.sum(jnp.where(iota(table.shape, 0) == index, table, 0.0), axis=0, keepdims=True)


def pad_rows(value, rows):
    if value.shape[0] == rows:
        return value
    return jnp.concatenate([value, jnp.zeros((rows - value.shape[0], value.shape[1]), value.dtype)], axis=0)


def exchange_kernel(
    cfg,
    slot_hbm,
    gate_hbm,
    tokens_hbm,
    grad_hbm,
    wg_hbm,
    wu_hbm,
    wd_hbm,
    gwg_ref,
    gwu_ref,
    gwd_ref,
    ret_ref,
    gsum_ref,
    where_ref,
    slot_ref,
    gate_ref,
    tokens,
    out_grad,
    wg,
    wu,
    wd,
    pick_send,
    pick_recv,
    pair_send_a,
    pair_send_b,
    pair_recv_a,
    pair_recv_b,
    z_own_a,
    z_own_b,
    z_send_a,
    z_send_b,
    z_recv_a,
    z_recv_b,
    hid_blocks,
    side_blocks,
    part_blocks,
    back_send,
    back_recv,
    local_sem,
    pick_ssem,
    pick_rsem,
    pair_ssem,
    pair_rsem,
    z_ssem,
    z_rsem,
    ag_ssem,
    fwd_ssem,
    ag_rsem,
    part_ssem,
    part_rsem,
    back_ssem,
    back_rsem,
):
    nx, nz, cap, flight, rb = cfg.nx, cfg.nz, cfg.cap, cfg.flight, cfg.rb
    half, width, fc, tok = cfg.half, cfg.width, cfg.fc, cfg.tok
    nd = 2 * nz
    me_x = lax.axis_index("expert")
    me_d = lax.axis_index("dp")
    my_z, my_c = me_d // 2, lax.rem(me_d, 2)
    other_c = 1 - my_c
    partner = my_z * 2 + other_c
    expert_here = me_x // GROUP

    x_peers = [lax.rem(me_x + k, nx) for k in range(1, nx)]
    z_peers = [lax.rem(my_z + k, nz) for k in range(1, nz)]
    d_peers = [lax.rem(me_d + k, nd) for k in range(1, nd)]
    barrier = pltpu.get_barrier_semaphore()
    for peer in x_peers:
        pl.semaphore_signal(barrier, inc=1, device_id=(me_d, peer), device_id_type=MESH)
    for peer in d_peers:
        pl.semaphore_signal(barrier, inc=1, device_id=(peer, me_x), device_id_type=MESH)

    pairs = (
        (slot_hbm, slot_ref),
        (gate_hbm, gate_ref),
        (tokens_hbm, tokens),
        (grad_hbm, out_grad),
        (wg_hbm.at[0], wg),
        (wu_hbm.at[0], wu),
        (wd_hbm.at[0], wd),
    )
    loads = [pltpu.make_async_copy(src, dst, local_sem.at[i]) for i, (src, dst) in enumerate(pairs)]
    for load in loads:
        load.start()

    def remote(src, dst, send_sem, recv_sem, target):
        return pltpu.make_async_remote_copy(
            src_ref=src,
            dst_ref=dst,
            send_sem=send_sem,
            recv_sem=recv_sem,
            device_id=target,
            device_id_type=MESH,
        )

    sends = []

    def launch(copy):
        copy.start()
        sends.append(copy)

    loads[0].wait()
    loads[1].wait()
    slots = slot_ref[...]
    picks = []
    for e in range(flight):
        where = local_index(slots[e : e + 1], me_x * tok, (me_x + 1) * tok, rb)
        where_ref[e] = where
        picks.append((where == iota((rb, tok), 1)).astype(F32).astype(BF16))
    loads[2].wait()
    loads[3].wait()
    for e in range(flight):
        rows = [mm(picks[e], tokens[...], 1, 0), mm(picks[e], out_grad[...], 1, 0)]
        pick_send[e] = jnp.concatenate(rows, axis=0).astype(BF16)
    pick_recv[me_x] = pick_send[expert_here]
    pl.semaphore_wait(barrier, len(x_peers) + len(d_peers))

    def pick_copy(k, peer, slot):
        return remote(
            pick_send.at[peer // GROUP], pick_recv.at[slot], pick_ssem.at[k], pick_rsem.at[slot], (me_d, peer)
        )

    for k, peer in enumerate(x_peers):
        launch(pick_copy(k, peer, me_x))

    slot_row = pick_row(slots.astype(F32), expert_here).astype(jnp.int32)
    gate_col = row_to_column(pick_row(gate_ref[...], expert_here))
    place_x, place_g = [], []
    empty = jnp.zeros((cap, rb), F32)
    for o in range(nx):
        mask = rank_mask(slot_row, o * tok, (o + 1) * tok, rb, 0).astype(F32)
        place_x += [mask, empty]
        place_g += [empty, mask]
    place = jnp.concatenate(
        [jnp.concatenate(place_x, axis=1), jnp.concatenate(place_g, axis=1)], axis=0
    ).astype(BF16)
    for k, peer in enumerate(x_peers):
        pick_copy(k, peer, peer).wait_recv()
    both = mm(place, pick_recv[...].reshape(nx * 2 * rb, fc), 1, 0)
    x = both[:cap].astype(BF16)
    scaled = (gate_col * both[cap:]).astype(BF16)
    grads = both[cap:].astype(BF16)

    def first_pair(core):
        cols = pl.ds(pl.multiple_of(core * half, half), half)
        return jnp.concatenate([mm(x, wg[:, cols], 1, 0), mm(x, wu[:, cols], 1, 0)], axis=0)

    def hidden_part(core):
        cols = pl.ds(pl.multiple_of(core * half, half), half)
        return mm(grads, wd[cols, :], 1, 1)

    def pair_copy(i):
        src, dst = ((pair_send_a, pair_recv_a), (pair_send_b, pair_recv_b))[i]
        return remote(src, dst, pair_ssem.at[i], pair_rsem.at[i], (partner, me_x))

    def z_copy(i, k, peer, slot):
        src, dst = ((z_send_a, z_recv_a), (z_send_b, z_recv_b))[i]
        return remote(
            src.at[peer], dst.at[slot], z_ssem.at[i, k], z_rsem.at[i, slot], (peer * 2 + my_c, me_x)
        )

    def z_start(i, own):
        got = (pair_recv_a, pair_recv_b)[i]
        send = (z_send_a, z_send_b)[i]
        keep = (z_own_a, z_own_b)[i]
        pair_copy(i).wait_recv()
        for j in range(nz):
            cols = slice(j * width, (j + 1) * width)
            total = own[:, cols] + got[:, cols]
            keep[j] = total
            send[j] = pad_rows(total, send.shape[1]).astype(BF16)
        for k, peer in enumerate(z_peers):
            launch(z_copy(i, k, peer, my_z))

    def z_finish(i):
        recv = (z_recv_a, z_recv_b)[i]
        total = (z_own_a, z_own_b)[i][my_z]
        for k, peer in enumerate(z_peers):
            z_copy(i, k, peer, peer).wait_recv()
            total = total + recv[peer].astype(F32)[: total.shape[0]]
        return total

    loads[4].wait()
    loads[5].wait()
    pair_send_a[...] = first_pair(other_c)
    launch(pair_copy(0))
    own_a = first_pair(my_c)
    z_start(0, own_a)
    loads[6].wait()
    pair_send_b[...] = hidden_part(other_c)
    launch(pair_copy(1))
    own_b = hidden_part(my_c)
    z_start(1, own_b)

    def ag_copy(i, owner, send_sem, target):
        block = (hid_blocks, side_blocks)[i].at[owner]
        return remote(block, block, send_sem, ag_rsem.at[i, owner], (target, me_x))

    def ag_start(i):
        for k, peer in enumerate(z_peers):
            launch(ag_copy(i, me_d, ag_ssem.at[i, k], peer * 2 + my_c))
        launch(ag_copy(i, me_d, fwd_ssem.at[i, 0], partner))

    def ag_forward(i):
        for k, peer in enumerate(z_peers):
            owner = peer * 2 + my_c
            ag_copy(i, owner, ag_ssem.at[i, k], owner).wait_recv()
            launch(ag_copy(i, owner, fwd_ssem.at[i, k + 1], partner))

    def ag_finish(i):
        for k, peer in enumerate([my_z] + z_peers):
            ag_copy(i, peer * 2 + other_c, fwd_ssem.at[i, k], partner).wait_recv()

    total = z_finish(0)
    pre_gate, pre_up = total[:cap], total[cap:]
    sig = 1.0 / (1.0 + jnp.exp(-pre_gate))
    silu = pre_gate * sig
    hidden = silu * pre_up
    hid_blocks[me_d] = pad_rows(hidden, cfg.rows_b).astype(BF16)
    ag_start(0)
    gate_slope = pre_up * sig * (1.0 + pre_gate * (1.0 - sig))
    upstream = z_finish(1)
    grad_hidden = gate_col * upstream
    side_blocks[me_d] = pad_rows(
        jnp.concatenate([grad_hidden * gate_slope, grad_hidden * silu], axis=0), cfg.rows_a
    ).astype(BF16)
    ag_start(1)
    gate_part = jnp.sum(hidden * upstream, axis=1, keepdims=True)
    lines = []
    for k in range(cfg.gate_rows):
        here = iota((cap, width), 0) == iota((cap, width), 1) + k * width
        lines.append(jnp.sum(jnp.where(here, gate_part, 0.0), axis=0, keepdims=True))
    part_blocks[me_d] = pad_rows(jnp.concatenate(lines, axis=0), cfg.part_rows)

    def part_copy(k, peer, slot):
        return remote(part_blocks.at[me_d], part_blocks.at[slot], part_ssem.at[k], part_rsem.at[slot], (peer, me_x))

    for k, peer in enumerate(d_peers):
        launch(part_copy(k, peer, me_d))

    ag_forward(0)

    def gather(blocks, core, start):
        parts = [blocks[j * 2 + core].astype(F32)[start : start + cap] for j in range(nz)]
        return jnp.concatenate(parts, axis=1).astype(BF16)

    def down_grad(core):
        rows = pl.ds(pl.multiple_of(core * half, half), half)
        gwd_ref[0, rows, :] = mm(gather(hid_blocks, core, 0), scaled, 0, 0).astype(BF16)

    down_grad(my_c)
    ag_forward(1)

    def back_half(core):
        cols = pl.ds(pl.multiple_of(core * half, half), half)
        gate_side, up_side = gather(side_blocks, core, 0), gather(side_blocks, core, cap)
        return gate_side, up_side, mm(gate_side, wg[:, cols], 1, 1) + mm(up_side, wu[:, cols], 1, 1)

    mine = back_half(my_c)
    ag_finish(0)
    ag_finish(1)
    others = back_half(other_c)
    back = (mine[2] + others[2]).astype(BF16)

    for k, peer in enumerate(d_peers):
        part_copy(k, peer, peer).wait_recv()
    gates_sum = sum(part_blocks[d] for d in range(nd))
    gate_lines = []
    for k in range(cfg.gate_rows):
        gate_lines += split_two(gates_sum[k : k + 1])
    lines = pad_rows(jnp.concatenate(gate_lines, axis=0), cfg.back_rows - rb)
    if width < fc:
        lines = jnp.concatenate([lines, jnp.zeros((lines.shape[0], fc - width), F32)], axis=1)
    for o in range(nx):
        mask = rank_mask(slot_row, o * tok, (o + 1) * tok, rb, 1).astype(F32).astype(BF16)
        back_send[o] = jnp.concatenate([mm(mask, back, 1, 0), lines], axis=0).astype(BF16)
    back_recv[me_x] = back_send[me_x]

    def back_copy(k, peer, slot):
        return remote(
            back_send.at[peer], back_recv.at[slot], back_ssem.at[k], back_rsem.at[slot], (me_d, peer)
        )

    for k, peer in enumerate(x_peers):
        launch(back_copy(k, peer, me_x))

    down_grad(other_c)
    for core, (gate_side, up_side, _) in ((my_c, mine), (other_c, others)):
        cols = pl.ds(pl.multiple_of(core * half, half), half)
        gwg_ref[0, :, cols] = mm(x, gate_side, 0, 0).astype(BF16)
        gwu_ref[0, :, cols] = mm(x, up_side, 0, 0).astype(BF16)
    for k, peer in enumerate(x_peers):
        back_copy(k, peer, peer).wait_recv()
    for e in range(flight):
        ret_ref[e] = sum(back_recv[e * GROUP + q, :rb].astype(F32) for q in range(GROUP))
    gsum_ref[...] = sum(
        back_recv[expert_here * GROUP + q, rb:].astype(F32)[:, :width] for q in range(GROUP)
    )
    for copy in sends:
        copy.wait_send()


def finish_kernel(
    cfg,
    gwg_ref,
    gwu_ref,
    gwd_ref,
    ret_ref,
    gsum_ref,
    where_ref,
    tok_out,
    wg_out,
    wu_out,
    wd_out,
    gates_out,
    tok_vmem,
    sem,
):
    copies = [
        pltpu.make_async_copy(src, dst, sem.at[i])
        for i, (src, dst) in enumerate(((gwg_ref, wg_out), (gwu_ref, wu_out), (gwd_ref, wd_out)))
    ]
    for copy in copies:
        copy.start()
    me_x = lax.axis_index("expert")
    total = None
    for e in range(cfg.flight):
        spread = (where_ref[e] == iota((cfg.rb, cfg.tok), 1)).astype(F32).astype(BF16)
        term = mm(spread, ret_ref[e].astype(BF16), 0, 0)
        total = term if total is None else total + term
    tok_vmem[...] = total.astype(BF16)
    copies.append(pltpu.make_async_copy(tok_vmem, tok_out, sem.at[3]))
    copies[3].start()
    wide = cfg.cap // GROUP
    first = lax.rem(me_x, GROUP) * wide
    gates = jnp.zeros((1, wide), F32)
    for k in range(cfg.gate_rows):
        line = gsum_ref[2 * k : 2 * k + 1, :] + gsum_ref[2 * k + 1 : 2 * k + 2, :]
        shape = (wide, cfg.width)
        here = iota(shape, 1) + k * cfg.width == iota(shape, 0) + first
        column = jnp.sum(jnp.where(here, line, 0.0), axis=1, keepdims=True)
        eye = iota((wide, wide), 0) == iota((wide, wide), 1)
        gates = gates + jnp.sum(jnp.where(eye, column, 0.0), axis=0, keepdims=True)
    gates_out[...] = gates
    for copy in copies:
        copy.wait()


class Sizes:
    pass


def per_device(mesh_shape, tokens, out_grad, slot_tokens, slot_gate, w_gate, w_up, w_down):
    c = Sizes()
    c.nx, nd = mesh_shape["expert"], mesh_shape["dp"]
    c.nz = nd // 2
    c.flight, c.cap = slot_tokens.shape
    c.tok, c.fc = tokens.shape
    ffq = w_gate.shape[2]
    c.half = ffq // 2
    c.width = c.half // c.nz
    most = 20
    c.rb = ceil_to(most, 8)
    c.gate_rows = ceil_to(c.cap, c.width) // c.width
    c.part_rows = ceil_to(c.gate_rows, 8)
    c.rows_a, c.rows_b = ceil_to(2 * c.cap, 16), ceil_to(c.cap, 16)
    c.back_rows = ceil_to(c.rb + 2 * c.gate_rows, 16)
    vmem = pl.BlockSpec(memory_space=pltpu.VMEM)
    hbm = pl.BlockSpec(memory_space=pltpu.HBM)
    dma = pltpu.SemaphoreType.DMA
    shape = jax.ShapeDtypeStruct
    grads = (
        shape((1, c.fc, ffq), BF16),
        shape((1, c.fc, ffq), BF16),
        shape((1, ffq, c.fc), BF16),
    )
    args = [
        pltpu.with_memory_space_constraint(value, pltpu.HBM)
        for value in (slot_tokens, slot_gate, tokens, out_grad, w_gate, w_up, w_down)
    ]
    parts = pl.pallas_call(
        functools.partial(exchange_kernel, c),
        out_shape=grads
        + (
            shape((c.flight, c.rb, c.fc), F32),
            shape((c.back_rows - c.rb, c.width), F32),
            shape((c.flight, c.rb, 1), jnp.int32),
        ),
        in_specs=[hbm] * 7,
        out_specs=[vmem] * 6,
        scratch_shapes=[
            pltpu.VMEM(slot_tokens.shape, jnp.int32),
            pltpu.VMEM(slot_gate.shape, F32),
            pltpu.VMEM((c.tok, c.fc), BF16),
            pltpu.VMEM((c.tok, c.fc), BF16),
            pltpu.VMEM((c.fc, ffq), BF16),
            pltpu.VMEM((c.fc, ffq), BF16),
            pltpu.VMEM((ffq, c.fc), BF16),
            pltpu.VMEM((c.flight, 2 * c.rb, c.fc), BF16),
            pltpu.VMEM((c.nx, 2 * c.rb, c.fc), BF16),
            pltpu.VMEM((2 * c.cap, c.half), F32),
            pltpu.VMEM((c.cap, c.half), F32),
            pltpu.VMEM((2 * c.cap, c.half), F32),
            pltpu.VMEM((c.cap, c.half), F32),
            pltpu.VMEM((c.nz, 2 * c.cap, c.width), F32),
            pltpu.VMEM((c.nz, c.cap, c.width), F32),
            pltpu.VMEM((c.nz, c.rows_a, c.width), BF16),
            pltpu.VMEM((c.nz, c.rows_b, c.width), BF16),
            pltpu.VMEM((c.nz, c.rows_a, c.width), BF16),
            pltpu.VMEM((c.nz, c.rows_b, c.width), BF16),
            pltpu.VMEM((nd, c.rows_b, c.width), BF16),
            pltpu.VMEM((nd, c.rows_a, c.width), BF16),
            pltpu.VMEM((nd, c.part_rows, c.width), F32),
            pltpu.VMEM((c.nx, c.back_rows, c.fc), BF16),
            pltpu.VMEM((c.nx, c.back_rows, c.fc), BF16),
            dma((7,)),
            dma((c.nx,)),
            dma((c.nx,)),
            dma((2,)),
            dma((2,)),
            dma((2, c.nz)),
            dma((2, c.nz)),
            dma((2, c.nz)),
            dma((2, c.nz)),
            dma((2, nd)),
            dma((nd,)),
            dma((nd,)),
            dma((c.nx,)),
            dma((c.nx,)),
        ],
        compiler_params=pltpu.CompilerParams(
            collective_id=0, has_side_effects=True, vmem_limit_bytes=40 * 1024 * 1024
        ),
        name="exchange",
    )(*args)

    return pl.pallas_call(
        functools.partial(finish_kernel, c),
        out_shape=(shape((c.tok, c.fc), BF16),) + grads + (shape((1, c.cap // GROUP), F32),),
        in_specs=[vmem] * 6,
        out_specs=[hbm] * 4 + [vmem],
        scratch_shapes=[pltpu.VMEM((c.tok, c.fc), BF16), dma((4,))],
        compiler_params=pltpu.CompilerParams(vmem_limit_bytes=40 * 1024 * 1024),
        name="finish",
    )(*parts)


def solution(mesh):
    in_specs = (
        P("expert", "dp"),
        P("expert", "dp"),
        P(),
        P(),
        P("expert", "dp", None),
        P("expert", "dp", None),
        P("expert", None, "dp"),
    )
    out_specs = (
        P("expert", "dp"),
        P("expert", "dp", None),
        P("expert", "dp", None),
        P("expert", None, "dp"),
        P("expert", None),
    )
    return jax.shard_map(
        functools.partial(per_device, dict(mesh.shape)),
        mesh=mesh,
        in_specs=in_specs,
        out_specs=out_specs,
        check_vma=False,
    )
```

```python
import functools

import jax
import jax.numpy as jnp
from jax import lax
from jax.experimental import pallas as pl
from jax.experimental.pallas import tpu as pltpu
from jax.sharding import PartitionSpec as P

GROUP = 4
MESH = pl.DeviceIdType.MESH
BF16 = jnp.bfloat16
F32 = jnp.float32
PIECES = 4


def ceil_to(value, step):
    return -(-value // step) * step


def mm(left, right, left_dim, right_dim):
    return lax.dot_general(
        left, right, (((left_dim,), (right_dim,)), ((), ())), preferred_element_type=F32
    )


def iota(shape, dim):
    return lax.broadcasted_iota(jnp.int32, shape, dim)


def count_below(row, bound):
    return jnp.sum(jnp.where(row < bound, 1.0, 0.0), axis=1, keepdims=True).astype(jnp.int32)


def rank_mask(row, low, high, rows, columns_dim):
    capacity = row.shape[1]
    start, end = count_below(row, low), count_below(row, high)
    shape = (rows, capacity) if columns_dim == 1 else (capacity, rows)
    slot, rank = iota(shape, columns_dim), iota(shape, 1 - columns_dim)
    return (slot == rank + start) & (slot < end)


def local_index(row, low, high, rows):
    mask = rank_mask(row, low, high, rows, 1)
    shifted = (row + (1 - low)).astype(F32)
    picked = jnp.sum(jnp.where(mask, shifted, 0.0), axis=1, keepdims=True)
    return picked.astype(jnp.int32) - 1


def row_to_column(row):
    size = row.shape[1]
    eye = iota((size, size), 0) == iota((size, size), 1)
    return jnp.sum(jnp.where(eye, row, 0.0), axis=1, keepdims=True)


def split_two(value):
    high = value.astype(BF16).astype(F32)
    return [high, value - high]


def pick_row(table, index):
    if table.shape[0] == 1:
        return table
    return jnp.sum(jnp.where(iota(table.shape, 0) == index, table, 0.0), axis=0, keepdims=True)


def pad_rows(value, rows):
    if value.shape[0] == rows:
        return value
    return jnp.concatenate([value, jnp.zeros((rows - value.shape[0], value.shape[1]), value.dtype)], axis=0)


def exchange_kernel(
    cfg,
    slot_hbm,
    gate_hbm,
    tokens_hbm,
    grad_hbm,
    wg_hbm,
    wu_hbm,
    wd_hbm,
    gwg_ref,
    gwu_ref,
    gwd_ref,
    ret_ref,
    gsum_ref,
    where_ref,
    slot_ref,
    gate_ref,
    tokens,
    out_grad,
    wg,
    wu,
    wd,
    pick_send,
    pick_recv,
    pair_send_a,
    pair_send_b,
    pair_recv_a,
    pair_recv_b,
    z_own_a,
    z_own_b,
    z_send_a,
    z_send_b,
    z_recv_a,
    z_recv_b,
    hid_blocks,
    side_blocks,
    part_blocks,
    back_send,
    back_recv,
    local_sem,
    pick_ssem,
    pick_rsem,
    pair_ssem,
    pair_rsem,
    z_ssem,
    z_rsem,
    ag_ssem,
    fwd_ssem,
    ag_rsem,
    part_ssem,
    part_rsem,
    back_ssem,
    back_rsem,
):
    nx, nz, cap, flight, rb = cfg.nx, cfg.nz, cfg.cap, cfg.flight, cfg.rb
    half, width, fc, tok = cfg.half, cfg.width, cfg.fc, cfg.tok
    nd = 2 * nz
    me_x = lax.axis_index("expert")
    me_d = lax.axis_index("dp")
    my_z, my_c = me_d // 2, lax.rem(me_d, 2)
    other_c = 1 - my_c
    partner = my_z * 2 + other_c
    expert_here = me_x // GROUP

    x_peers = [lax.rem(me_x + k, nx) for k in range(1, nx)]
    z_peers = [lax.rem(my_z + k, nz) for k in range(1, nz)]
    d_peers = [lax.rem(me_d + k, nd) for k in range(1, nd)]
    barrier = pltpu.get_barrier_semaphore()
    for peer in x_peers:
        pl.semaphore_signal(barrier, inc=1, device_id=(me_d, peer), device_id_type=MESH)
    for peer in d_peers:
        pl.semaphore_signal(barrier, inc=1, device_id=(peer, me_x), device_id_type=MESH)

    pairs = (
        (slot_hbm, slot_ref),
        (gate_hbm, gate_ref),
        (tokens_hbm, tokens),
        (grad_hbm, out_grad),
        (wg_hbm.at[0], wg),
        (wu_hbm.at[0], wu),
        (wd_hbm.at[0], wd),
    )
    loads = [pltpu.make_async_copy(src, dst, local_sem.at[i]) for i, (src, dst) in enumerate(pairs)]
    for load in loads:
        load.start()

    def remote(src, dst, send_sem, recv_sem, target):
        return pltpu.make_async_remote_copy(
            src_ref=src,
            dst_ref=dst,
            send_sem=send_sem,
            recv_sem=recv_sem,
            device_id=target,
            device_id_type=MESH,
        )

    sends = []

    def launch(copy):
        copy.start()
        sends.append(copy)

    loads[0].wait()
    loads[1].wait()
    slots = slot_ref[...]
    picks = []
    for e in range(flight):
        where = local_index(slots[e : e + 1], me_x * tok, (me_x + 1) * tok, rb)
        where_ref[e] = where
        picks.append((where == iota((rb, tok), 1)).astype(F32).astype(BF16))
    def pick_copy(i, k, peer, slot):
        return remote(
            pick_send.at[peer // GROUP, i],
            pick_recv.at[slot, i],
            pick_ssem.at[i, k],
            pick_rsem.at[i, slot],
            (me_d, peer),
        )

    for i, source in enumerate((tokens, out_grad)):
        loads[2 + i].wait()
        for e in range(flight):
            rows = mm(picks[e], source[...], 1, 0)
            if cfg.fold_pick:
                rows = jnp.concatenate([rows[:, : fc // 2], rows[:, fc // 2 :]], axis=0)
            pick_send[e, i] = pad_rows(rows, pick_send.shape[2]).astype(BF16)
        if i == 0:
            pl.semaphore_wait(barrier, len(x_peers) + len(d_peers))
        for k, peer in enumerate(x_peers):
            launch(pick_copy(i, k, peer, me_x))
    pick_recv[me_x] = pick_send[expert_here]

    slot_row = pick_row(slots.astype(F32), expert_here).astype(jnp.int32)
    gate_col = row_to_column(pick_row(gate_ref[...], expert_here))
    place_rows = [[], []]
    empty = jnp.zeros((cap, pick_recv.shape[2] - rb), F32)
    for o in range(nx):
        mask = rank_mask(slot_row, o * tok, (o + 1) * tok, rb, 0).astype(F32)
        place_rows[0] += [mask, empty]
        place_rows[1] += [empty, mask]
    place = [jnp.concatenate(blocks, axis=1) for blocks in place_rows[: 2 if cfg.fold_pick else 1]]
    place = jnp.concatenate(place, axis=0).astype(BF16)

    def placed(i):
        for k, peer in enumerate(x_peers):
            pick_copy(i, k, peer, peer).wait_recv()
        rows = jnp.concatenate([pick_recv[o, i] for o in range(nx)], axis=0)
        value = mm(place, rows, 1, 0)
        if cfg.fold_pick:
            value = jnp.concatenate([value[:cap], value[cap:]], axis=1)
        return value

    x = placed(0).astype(BF16)

    fold_b = cfg.fold_b

    def pack_b(value):
        if fold_b:
            value = jnp.concatenate([value[:, : width // 2], value[:, width // 2 :]], axis=0)
        return pad_rows(value, cfg.rows_b).astype(BF16)

    def unpack_b(block):
        block = block.astype(F32)
        if fold_b:
            return jnp.concatenate([block[:cap], block[cap : 2 * cap]], axis=1)
        return block[:cap]

    def pack_a(value):
        return pad_rows(value, cfg.rows_a).astype(BF16)

    def unpack_a(block):
        return block.astype(F32)[: 2 * cap]

    def first_pair(core):
        cols = pl.ds(pl.multiple_of(core * half, half), half)
        return jnp.concatenate([mm(x, wg[:, cols], 1, 0), mm(x, wu[:, cols], 1, 0)], axis=0)

    def hidden_part(core):
        cols = pl.ds(pl.multiple_of(core * half, half), half)
        return mm(grads, wd[cols, :], 1, 1)

    def pair_copy(i):
        src, dst = ((pair_send_a, pair_recv_a), (pair_send_b, pair_recv_b))[i]
        return remote(src, dst, pair_ssem.at[i], pair_rsem.at[i], (partner, me_x))

    def z_copy(i, k, peer, slot):
        src, dst = ((z_send_a, z_recv_a), (z_send_b, z_recv_b))[i]
        return remote(
            src.at[peer], dst.at[slot], z_ssem.at[i, k], z_rsem.at[i, slot], (peer * 2 + my_c, me_x)
        )

    def z_start(i, own):
        got = (pair_recv_a, pair_recv_b)[i]
        send = (z_send_a, z_send_b)[i]
        keep = (z_own_a, z_own_b)[i]
        pair_copy(i).wait_recv()
        for j in range(nz):
            cols = slice(j * width, (j + 1) * width)
            total = own[:, cols] + got[:, cols]
            keep[j] = total
            send[j] = (pack_a, pack_b)[i](total)
        for k, peer in enumerate(z_peers):
            launch(z_copy(i, k, peer, my_z))

    def z_finish(i):
        recv = (z_recv_a, z_recv_b)[i]
        total = (z_own_a, z_own_b)[i][my_z]
        for k, peer in enumerate(z_peers):
            z_copy(i, k, peer, peer).wait_recv()
            total = total + (unpack_a, unpack_b)[i](recv[peer])
        return total

    loads[4].wait()
    loads[5].wait()
    pair_send_a[...] = first_pair(other_c)
    launch(pair_copy(0))
    own_a = first_pair(my_c)
    grads = placed(1)
    scaled = (gate_col * grads).astype(BF16)
    grads = grads.astype(BF16)
    z_start(0, own_a)
    loads[6].wait()
    pair_send_b[...] = hidden_part(other_c)
    launch(pair_copy(1))
    own_b = hidden_part(my_c)
    z_start(1, own_b)

    def ag_copy(i, owner, send_sem, target):
        block = (hid_blocks, side_blocks)[i].at[owner]
        return remote(block, block, send_sem, ag_rsem.at[i, owner], (target, me_x))

    def ag_start(i):
        for k, peer in enumerate(z_peers):
            launch(ag_copy(i, me_d, ag_ssem.at[i, k], peer * 2 + my_c))
        launch(ag_copy(i, me_d, fwd_ssem.at[i, 0], partner))

    def ag_forward(i, k):
        owner = z_peers[k] * 2 + my_c
        ag_copy(i, owner, ag_ssem.at[i, k], owner).wait_recv()
        launch(ag_copy(i, owner, fwd_ssem.at[i, k + 1], partner))

    def ag_finish(i, k):
        owner = ([my_z] + z_peers)[k] * 2 + other_c
        ag_copy(i, owner, fwd_ssem.at[i, k], partner).wait_recv()

    total = z_finish(0)
    pre_gate, pre_up = total[:cap], total[cap:]
    sig = 1.0 / (1.0 + jnp.exp(-pre_gate))
    silu = pre_gate * sig
    hidden = silu * pre_up
    hid_blocks[me_d] = pack_b(hidden)
    ag_start(0)
    gate_slope = pre_up * sig * (1.0 + pre_gate * (1.0 - sig))
    upstream = z_finish(1)
    grad_hidden = gate_col * upstream
    side_blocks[me_d] = pack_a(jnp.concatenate([grad_hidden * gate_slope, grad_hidden * silu], axis=0))
    ag_start(1)
    gate_part = jnp.sum(hidden * upstream, axis=1, keepdims=True)
    lines = []
    for k in range(cfg.gate_rows):
        here = iota((cap, width), 0) == iota((cap, width), 1) + k * width
        lines.append(jnp.sum(jnp.where(here, gate_part, 0.0), axis=0, keepdims=True))
    part_blocks[me_d] = pad_rows(jnp.concatenate(lines, axis=0), cfg.part_rows)

    def part_copy(k, peer, slot):
        return remote(part_blocks.at[me_d], part_blocks.at[slot], part_ssem.at[k], part_rsem.at[slot], (peer, me_x))

    for k, peer in enumerate(d_peers):
        launch(part_copy(k, peer, me_d))

    def unit_start(core, zs):
        start = core * half
        if len(zs) == 1:
            start = start + zs[0] * width
        size = len(zs) * width
        return pl.ds(pl.multiple_of(start, size), size)

    def unit_sides(core, zs):
        blocks = [unpack_a(side_blocks[z * 2 + core]) for z in zs]
        return [
            jnp.concatenate([block[i * cap : (i + 1) * cap] for block in blocks], axis=1).astype(BF16)
            for i in range(2)
        ]

    def unit_back(core, zs):
        cols = unit_start(core, zs)
        gate_side, up_side = unit_sides(core, zs)
        return mm(gate_side, wg[:, cols], 1, 1) + mm(up_side, wu[:, cols], 1, 1)

    def unit_grads(core, zs):
        cols = unit_start(core, zs)
        gate_side, up_side = unit_sides(core, zs)
        hid = [unpack_b(hid_blocks[z * 2 + core]) for z in zs]
        hid = jnp.concatenate(hid, axis=1).astype(BF16)
        gwd_ref[0, cols, :] = mm(hid, scaled, 0, 0).astype(BF16)
        gwg_ref[0, :, cols] = mm(x, gate_side, 0, 0).astype(BF16)
        gwu_ref[0, :, cols] = mm(x, up_side, 0, 0).astype(BF16)

    for k in range(nz - 1):
        ag_forward(0, k)
    if width % 128 == 0:
        back = unit_back(my_c, [my_z])
        unit_grads(my_c, [my_z])
        ag_finish(0, 0)
        ag_finish(1, 0)
        back = back + unit_back(other_c, [my_z])
        unit_grads(other_c, [my_z])
        late = []
        for k, peer in enumerate(z_peers):
            ag_forward(1, k)
            back = back + unit_back(my_c, [peer])
            if k + 1 < len(z_peers):
                unit_grads(my_c, [peer])
            else:
                late.append((my_c, [peer]))
        for k, peer in enumerate(z_peers):
            ag_finish(0, k + 1)
            ag_finish(1, k + 1)
            back = back + unit_back(other_c, [peer])
            late.append((other_c, [peer]))
    else:
        for k in range(nz - 1):
            ag_forward(1, k)
        back = unit_back(my_c, list(range(nz)))
        for k in range(nz):
            ag_finish(0, k)
            ag_finish(1, k)
        back = back + unit_back(other_c, list(range(nz)))
        late = [(my_c, list(range(nz))), (other_c, list(range(nz)))]
    back = back.astype(BF16)

    for k, peer in enumerate(d_peers):
        part_copy(k, peer, peer).wait_recv()
    gates_sum = sum(part_blocks[d] for d in range(nd))
    gate_lines = []
    for k in range(cfg.gate_rows):
        gate_lines += split_two(gates_sum[k : k + 1])
    lines = pad_rows(jnp.concatenate(gate_lines, axis=0), cfg.back_rows - rb)
    if width < fc:
        lines = jnp.concatenate([lines, jnp.zeros((lines.shape[0], fc - width), F32)], axis=1)
    for o in range(nx):
        mask = rank_mask(slot_row, o * tok, (o + 1) * tok, rb, 1).astype(F32).astype(BF16)
        back_send[o] = jnp.concatenate([mm(mask, back, 1, 0), lines], axis=0).astype(BF16)
    back_recv[me_x] = back_send[me_x]

    def back_copy(k, peer, slot):
        return remote(
            back_send.at[peer], back_recv.at[slot], back_ssem.at[k], back_rsem.at[slot], (me_d, peer)
        )

    for k, peer in enumerate(x_peers):
        launch(back_copy(k, peer, me_x))

    for core, zs in late:
        unit_grads(core, zs)
    for k, peer in enumerate(x_peers):
        back_copy(k, peer, peer).wait_recv()
    for e in range(flight):
        ret_ref[e] = sum(back_recv[e * GROUP + q, :rb].astype(F32) for q in range(GROUP))
    gsum_ref[...] = sum(
        back_recv[expert_here * GROUP + q, rb:].astype(F32)[:, :width] for q in range(GROUP)
    )
    for copy in sends:
        copy.wait_send()


def pieces(rows):
    step = rows // PIECES
    return [pl.ds(j * step, step) for j in range(PIECES)]


def finish_kernel(
    cfg,
    gwg_ref,
    gwu_ref,
    gwd_ref,
    ret_ref,
    gsum_ref,
    where_ref,
    tok_out,
    wg_out,
    wu_out,
    wd_out,
    gates_out,
    tok_vmem,
    sem,
):
    copies = [
        pltpu.make_async_copy(src.at[:, rows], dst.at[:, rows], sem.at[i, j])
        for i, (src, dst) in enumerate(((gwg_ref, wg_out), (gwu_ref, wu_out), (gwd_ref, wd_out)))
        for j, rows in enumerate(pieces(src.shape[1]))
    ]
    for copy in copies:
        copy.start()
    me_x = lax.axis_index("expert")
    total = None
    for e in range(cfg.flight):
        spread = (where_ref[e] == iota((cfg.rb, cfg.tok), 1)).astype(F32).astype(BF16)
        term = mm(spread, ret_ref[e].astype(BF16), 0, 0)
        total = term if total is None else total + term
    tok_vmem[...] = total.astype(BF16)
    copies.append(pltpu.make_async_copy(tok_vmem, tok_out, sem.at[3, 0]))
    copies[-1].start()
    wide = cfg.cap // GROUP
    first = lax.rem(me_x, GROUP) * wide
    gates = jnp.zeros((1, wide), F32)
    for k in range(cfg.gate_rows):
        line = gsum_ref[2 * k : 2 * k + 1, :] + gsum_ref[2 * k + 1 : 2 * k + 2, :]
        shape = (wide, cfg.width)
        here = iota(shape, 1) + k * cfg.width == iota(shape, 0) + first
        column = jnp.sum(jnp.where(here, line, 0.0), axis=1, keepdims=True)
        eye = iota((wide, wide), 0) == iota((wide, wide), 1)
        gates = gates + jnp.sum(jnp.where(eye, column, 0.0), axis=0, keepdims=True)
    gates_out[...] = gates
    for copy in copies:
        copy.wait()


class Sizes:
    pass


def per_device(mesh_shape, tokens, out_grad, slot_tokens, slot_gate, w_gate, w_up, w_down):
    c = Sizes()
    c.nx, nd = mesh_shape["expert"], mesh_shape["dp"]
    c.nz = nd // 2
    c.flight, c.cap = slot_tokens.shape
    c.tok, c.fc = tokens.shape
    ffq = w_gate.shape[2]
    c.half = ffq // 2
    c.width = c.half // c.nz
    most = 20
    c.rb = ceil_to(most, 8)
    c.gate_rows = ceil_to(c.cap, c.width) // c.width
    c.part_rows = ceil_to(c.gate_rows, 8)
    c.fold_b, c.fold_pick = c.width % 256 == 0, c.fc % 256 == 0
    c.rows_a = ceil_to(2 * c.cap, 16)
    c.rows_b, cols_b = (c.rows_a, c.width // 2) if c.fold_b else (ceil_to(c.cap, 16), c.width)
    pick = (ceil_to(2 * c.rb, 16), c.fc // 2) if c.fold_pick else (ceil_to(c.rb, 16), c.fc)
    c.back_rows = ceil_to(c.rb + 2 * c.gate_rows, 16)
    vmem = pl.BlockSpec(memory_space=pltpu.VMEM)
    hbm = pl.BlockSpec(memory_space=pltpu.HBM)
    dma = pltpu.SemaphoreType.DMA
    shape = jax.ShapeDtypeStruct
    grads = (
        shape((1, c.fc, ffq), BF16),
        shape((1, c.fc, ffq), BF16),
        shape((1, ffq, c.fc), BF16),
    )
    args = [
        pltpu.with_memory_space_constraint(value, pltpu.HBM)
        for value in (slot_tokens, slot_gate, tokens, out_grad, w_gate, w_up, w_down)
    ]
    parts = pl.pallas_call(
        functools.partial(exchange_kernel, c),
        out_shape=grads
        + (
            shape((c.flight, c.rb, c.fc), F32),
            shape((c.back_rows - c.rb, c.width), F32),
            shape((c.flight, c.rb, 1), jnp.int32),
        ),
        in_specs=[hbm] * 7,
        out_specs=[vmem] * 6,
        scratch_shapes=[
            pltpu.VMEM(slot_tokens.shape, jnp.int32),
            pltpu.VMEM(slot_gate.shape, F32),
            pltpu.VMEM((c.tok, c.fc), BF16),
            pltpu.VMEM((c.tok, c.fc), BF16),
            pltpu.VMEM((c.fc, ffq), BF16),
            pltpu.VMEM((c.fc, ffq), BF16),
            pltpu.VMEM((ffq, c.fc), BF16),
            pltpu.VMEM((c.flight, 2) + pick, BF16),
            pltpu.VMEM((c.nx, 2) + pick, BF16),
            pltpu.VMEM((2 * c.cap, c.half), F32),
            pltpu.VMEM((c.cap, c.half), F32),
            pltpu.VMEM((2 * c.cap, c.half), F32),
            pltpu.VMEM((c.cap, c.half), F32),
            pltpu.VMEM((c.nz, 2 * c.cap, c.width), F32),
            pltpu.VMEM((c.nz, c.cap, c.width), F32),
            pltpu.VMEM((c.nz, c.rows_a, c.width), BF16),
            pltpu.VMEM((c.nz, c.rows_b, cols_b), BF16),
            pltpu.VMEM((c.nz, c.rows_a, c.width), BF16),
            pltpu.VMEM((c.nz, c.rows_b, cols_b), BF16),
            pltpu.VMEM((nd, c.rows_b, cols_b), BF16),
            pltpu.VMEM((nd, c.rows_a, c.width), BF16),
            pltpu.VMEM((nd, c.part_rows, c.width), F32),
            pltpu.VMEM((c.nx, c.back_rows, c.fc), BF16),
            pltpu.VMEM((c.nx, c.back_rows, c.fc), BF16),
            dma((7,)),
            dma((2, c.nx)),
            dma((2, c.nx)),
            dma((2,)),
            dma((2,)),
            dma((2, c.nz)),
            dma((2, c.nz)),
            dma((2, c.nz)),
            dma((2, c.nz)),
            dma((2, nd)),
            dma((nd,)),
            dma((nd,)),
            dma((c.nx,)),
            dma((c.nx,)),
        ],
        compiler_params=pltpu.CompilerParams(
            collective_id=0, has_side_effects=True, vmem_limit_bytes=40 * 1024 * 1024
        ),
        name="exchange",
    )(*args)

    return pl.pallas_call(
        functools.partial(finish_kernel, c),
        out_shape=(shape((c.tok, c.fc), BF16),) + grads + (shape((1, c.cap // GROUP), F32),),
        in_specs=[vmem] * 6,
        out_specs=[hbm] * 4 + [vmem],
        scratch_shapes=[pltpu.VMEM((c.tok, c.fc), BF16), dma((4, PIECES))],
        compiler_params=pltpu.CompilerParams(vmem_limit_bytes=40 * 1024 * 1024),
        name="finish",
    )(*parts)


def solution(mesh):
    in_specs = (
        P("expert", "dp"),
        P("expert", "dp"),
        P(),
        P(),
        P("expert", "dp", None),
        P("expert", "dp", None),
        P("expert", None, "dp"),
    )
    out_specs = (
        P("expert", "dp"),
        P("expert", "dp", None),
        P("expert", "dp", None),
        P("expert", None, "dp"),
        P("expert", None),
    )
    return jax.shard_map(
        functools.partial(per_device, dict(mesh.shape)),
        mesh=mesh,
        in_specs=in_specs,
        out_specs=out_specs,
        check_vma=False,
    )
```

```python
import functools

import jax
import jax.numpy as jnp
from jax import lax
from jax.experimental import pallas as pl
from jax.experimental.pallas import tpu as pltpu
from jax.sharding import PartitionSpec as P

GROUP = 4
MESH = pl.DeviceIdType.MESH
BF16 = jnp.bfloat16
F32 = jnp.float32
PIECES = 4


def ceil_to(value, step):
    return -(-value // step) * step


def mm(left, right, left_dim, right_dim):
    return lax.dot_general(
        left, right, (((left_dim,), (right_dim,)), ((), ())), preferred_element_type=F32
    )


def iota(shape, dim):
    return lax.broadcasted_iota(jnp.int32, shape, dim)


def count_below(row, bound):
    return jnp.sum(jnp.where(row < bound, 1.0, 0.0), axis=1, keepdims=True).astype(jnp.int32)


def rank_mask(row, low, high, rows, columns_dim):
    capacity = row.shape[1]
    start, end = count_below(row, low), count_below(row, high)
    shape = (rows, capacity) if columns_dim == 1 else (capacity, rows)
    slot, rank = iota(shape, columns_dim), iota(shape, 1 - columns_dim)
    return (slot == rank + start) & (slot < end)


def local_index(row, low, high, rows):
    mask = rank_mask(row, low, high, rows, 1)
    shifted = (row + (1 - low)).astype(F32)
    picked = jnp.sum(jnp.where(mask, shifted, 0.0), axis=1, keepdims=True)
    return picked.astype(jnp.int32) - 1


def row_to_column(row):
    size = row.shape[1]
    eye = iota((size, size), 0) == iota((size, size), 1)
    return jnp.sum(jnp.where(eye, row, 0.0), axis=1, keepdims=True)


def split_two(value):
    high = value.astype(BF16).astype(F32)
    return [high, value - high]


def pick_row(table, index):
    if table.shape[0] == 1:
        return table
    return jnp.sum(jnp.where(iota(table.shape, 0) == index, table, 0.0), axis=0, keepdims=True)


def pad_rows(value, rows):
    if value.shape[0] == rows:
        return value
    return jnp.concatenate([value, jnp.zeros((rows - value.shape[0], value.shape[1]), value.dtype)], axis=0)


def across(place, offset, bits):
    for bit in bits:
        if offset & bit:
            place = place + bit * (1 - 2 * lax.rem(place // bit, 2))
    return place


def exchange_kernel(
    cfg,
    slot_hbm,
    gate_hbm,
    tokens_hbm,
    grad_hbm,
    wg_hbm,
    wu_hbm,
    wd_hbm,
    gwg_ref,
    gwu_ref,
    gwd_ref,
    ret_ref,
    gsum_ref,
    where_ref,
    slot_ref,
    gate_ref,
    tokens,
    out_grad,
    wg,
    wu,
    wd,
    pick_send,
    pick_recv,
    pair_send_a,
    pair_send_b,
    pair_recv_a,
    pair_recv_b,
    z_own_a,
    z_own_b,
    z_send_a,
    z_send_b,
    z_recv_a,
    z_recv_b,
    hid_blocks,
    side_blocks,
    part_blocks,
    back_send,
    back_recv,
    local_sem,
    pick_ssem,
    pick_rsem,
    pair_ssem,
    pair_rsem,
    z_ssem,
    z_rsem,
    ag_ssem,
    fwd_ssem,
    ag_rsem,
    part_ssem,
    part_rsem,
    back_ssem,
    back_rsem,
):
    nx, nz, cap, flight, rb = cfg.nx, cfg.nz, cfg.cap, cfg.flight, cfg.rb
    half, width, fc, tok = cfg.half, cfg.width, cfg.fc, cfg.tok
    nd = 2 * nz
    me_x = lax.axis_index("expert")
    me_d = lax.axis_index("dp")
    my_z, my_c = me_d // 2, lax.rem(me_d, 2)
    other_c = 1 - my_c
    partner = my_z * 2 + other_c
    expert_here = me_x // GROUP

    x_peers = [lax.rem(me_x + k, nx) for k in range(1, nx)]
    z_peers = [lax.rem(my_z + k, nz) for k in range(1, nz)]
    d_peers = [lax.rem(me_d + k, nd) for k in range(1, nd)]
    barrier = pltpu.get_barrier_semaphore()
    for peer in x_peers:
        pl.semaphore_signal(barrier, inc=1, device_id=(me_d, peer), device_id_type=MESH)
    for peer in d_peers:
        pl.semaphore_signal(barrier, inc=1, device_id=(peer, me_x), device_id_type=MESH)

    pairs = (
        (slot_hbm, slot_ref),
        (gate_hbm, gate_ref),
        (tokens_hbm, tokens),
        (grad_hbm, out_grad),
        (wg_hbm.at[0], wg),
        (wu_hbm.at[0], wu),
        (wd_hbm.at[0], wd),
    )
    loads = [pltpu.make_async_copy(src, dst, local_sem.at[i]) for i, (src, dst) in enumerate(pairs)]
    for load in loads:
        load.start()

    def remote(src, dst, send_sem, recv_sem, target):
        return pltpu.make_async_remote_copy(
            src_ref=src,
            dst_ref=dst,
            send_sem=send_sem,
            recv_sem=recv_sem,
            device_id=target,
            device_id_type=MESH,
        )

    sends = []

    def launch(copy):
        copy.start()
        sends.append(copy)

    loads[0].wait()
    loads[1].wait()
    slots = slot_ref[...]
    picks = []
    for e in range(flight):
        where = local_index(slots[e : e + 1], me_x * tok, (me_x + 1) * tok, rb)
        where_ref[e] = where
        picks.append((where == iota((rb, tok), 1)).astype(F32).astype(BF16))
    def pick_copy(i, k, peer, slot):
        return remote(
            pick_send.at[peer // GROUP, i],
            pick_recv.at[slot, i],
            pick_ssem.at[i, k],
            pick_rsem.at[i, slot],
            (me_d, peer),
        )

    for i, source in enumerate((tokens, out_grad)):
        loads[2 + i].wait()
        for e in range(flight):
            rows = mm(picks[e], source[...], 1, 0)
            if cfg.fold_pick:
                rows = jnp.concatenate([rows[:, : fc // 2], rows[:, fc // 2 :]], axis=0)
            pick_send[e, i] = pad_rows(rows, pick_send.shape[2]).astype(BF16)
        if i == 0:
            pl.semaphore_wait(barrier, len(x_peers) + len(d_peers))
        for k, peer in enumerate(x_peers):
            launch(pick_copy(i, k, peer, me_x))
    pick_recv[me_x] = pick_send[expert_here]

    slot_row = pick_row(slots.astype(F32), expert_here).astype(jnp.int32)
    gate_col = row_to_column(pick_row(gate_ref[...], expert_here))
    place_rows = [[], []]
    empty = jnp.zeros((cap, pick_recv.shape[2] - rb), F32)
    for o in range(nx):
        mask = rank_mask(slot_row, o * tok, (o + 1) * tok, rb, 0).astype(F32)
        place_rows[0] += [mask, empty]
        place_rows[1] += [empty, mask]
    place = [jnp.concatenate(blocks, axis=1) for blocks in place_rows[: 2 if cfg.fold_pick else 1]]
    place = jnp.concatenate(place, axis=0).astype(BF16)

    def placed(i):
        for k, peer in enumerate(x_peers):
            pick_copy(i, k, peer, peer).wait_recv()
        rows = jnp.concatenate([pick_recv[o, i] for o in range(nx)], axis=0)
        value = mm(place, rows, 1, 0)
        if cfg.fold_pick:
            value = jnp.concatenate([value[:cap], value[cap:]], axis=1)
        return value

    x = placed(0).astype(BF16)

    fold_b = cfg.fold_b

    def pack_b(value):
        if fold_b:
            value = jnp.concatenate([value[:, : width // 2], value[:, width // 2 :]], axis=0)
        return pad_rows(value, cfg.rows_b).astype(BF16)

    def unpack_b(block):
        block = block.astype(F32)
        if fold_b:
            return jnp.concatenate([block[:cap], block[cap : 2 * cap]], axis=1)
        return block[:cap]

    def pack_a(value):
        return pad_rows(value, cfg.rows_a).astype(BF16)

    def unpack_a(block):
        return block.astype(F32)[: 2 * cap]

    def first_pair(core):
        cols = pl.ds(pl.multiple_of(core * half, half), half)
        return jnp.concatenate([mm(x, wg[:, cols], 1, 0), mm(x, wu[:, cols], 1, 0)], axis=0)

    def hidden_part(core):
        cols = pl.ds(pl.multiple_of(core * half, half), half)
        return mm(grads, wd[cols, :], 1, 1)

    def pair_copy(i):
        src, dst = ((pair_send_a, pair_recv_a), (pair_send_b, pair_recv_b))[i]
        return remote(src, dst, pair_ssem.at[i], pair_rsem.at[i], (partner, me_x))

    def z_copy(i, k, peer, slot):
        src, dst = ((z_send_a, z_recv_a), (z_send_b, z_recv_b))[i]
        return remote(
            src.at[peer], dst.at[slot], z_ssem.at[i, k], z_rsem.at[i, slot], (peer * 2 + my_c, me_x)
        )

    def z_start(i, own):
        got = (pair_recv_a, pair_recv_b)[i]
        send = (z_send_a, z_send_b)[i]
        keep = (z_own_a, z_own_b)[i]
        pair_copy(i).wait_recv()
        for j in range(nz):
            cols = slice(j * width, (j + 1) * width)
            total = own[:, cols] + got[:, cols]
            keep[j] = total
            send[j] = (pack_a, pack_b)[i](total)
        for k, peer in enumerate(z_peers):
            launch(z_copy(i, k, peer, my_z))

    def z_finish(i):
        recv = (z_recv_a, z_recv_b)[i]
        total = (z_own_a, z_own_b)[i][my_z]
        for k, peer in enumerate(z_peers):
            z_copy(i, k, peer, peer).wait_recv()
            total = total + (unpack_a, unpack_b)[i](recv[peer])
        return total

    loads[4].wait()
    loads[5].wait()
    pair_send_a[...] = first_pair(other_c)
    launch(pair_copy(0))
    own_a = first_pair(my_c)
    grads = placed(1)
    scaled = (gate_col * grads).astype(BF16)
    grads = grads.astype(BF16)
    z_start(0, own_a)
    loads[6].wait()
    pair_send_b[...] = hidden_part(other_c)
    launch(pair_copy(1))
    own_b = hidden_part(my_c)
    z_start(1, own_b)

    def ag_copy(i, owner, send_sem, target):
        block = (hid_blocks, side_blocks)[i].at[owner]
        return remote(block, block, send_sem, ag_rsem.at[i, owner], (target, me_x))

    bits = [2**k for k in range(nz.bit_length() - 1)]
    offsets = sorted(range(1, nz), key=lambda o: (bin(o).count("1"), -o))
    chips = [across(my_z, o, bits) for o in offsets]

    def ag_spread(i, offset, slot):
        owner = across(my_z, offset, bits) * 2 + my_c
        for k, bit in enumerate(bits):
            if offset == 0 or bit < (offset & -offset):
                launch(ag_copy(i, owner, ag_ssem.at[i, slot, k], across(my_z, bit, bits) * 2 + my_c))
        launch(ag_copy(i, owner, fwd_ssem.at[i, slot], partner))

    def ag_start(i):
        ag_spread(i, 0, 0)

    def ag_forward(i, k):
        low = offsets[k] & -offsets[k]
        source = across(my_z, low, bits) * 2 + my_c
        ag_copy(i, chips[k] * 2 + my_c, ag_ssem.at[i, 0, 0], source).wait_recv()
        ag_spread(i, offsets[k], k + 1)

    def ag_finish(i, k):
        owner = ([my_z] + chips)[k] * 2 + other_c
        ag_copy(i, owner, fwd_ssem.at[i, k], partner).wait_recv()

    total = z_finish(0)
    pre_gate, pre_up = total[:cap], total[cap:]
    sig = 1.0 / (1.0 + jnp.exp(-pre_gate))
    silu = pre_gate * sig
    hidden = silu * pre_up
    hid_blocks[me_d] = pack_b(hidden)
    ag_start(0)
    gate_slope = pre_up * sig * (1.0 + pre_gate * (1.0 - sig))
    upstream = z_finish(1)
    grad_hidden = gate_col * upstream
    side_blocks[me_d] = pack_a(jnp.concatenate([grad_hidden * gate_slope, grad_hidden * silu], axis=0))
    ag_start(1)
    gate_part = jnp.sum(hidden * upstream, axis=1, keepdims=True)
    lines = []
    for k in range(cfg.gate_rows):
        here = iota((cap, width), 0) == iota((cap, width), 1) + k * width
        lines.append(jnp.sum(jnp.where(here, gate_part, 0.0), axis=0, keepdims=True))
    part_blocks[me_d] = pad_rows(jnp.concatenate(lines, axis=0), cfg.part_rows)

    def part_copy(k, peer, slot):
        return remote(part_blocks.at[me_d], part_blocks.at[slot], part_ssem.at[k], part_rsem.at[slot], (peer, me_x))

    for k, peer in enumerate(d_peers):
        launch(part_copy(k, peer, me_d))

    def unit_start(core, zs):
        start = core * half
        if len(zs) == 1:
            start = start + zs[0] * width
        size = len(zs) * width
        return pl.ds(pl.multiple_of(start, size), size)

    def unit_sides(core, zs):
        blocks = [unpack_a(side_blocks[z * 2 + core]) for z in zs]
        return [
            jnp.concatenate([block[i * cap : (i + 1) * cap] for block in blocks], axis=1).astype(BF16)
            for i in range(2)
        ]

    def unit_back(core, zs):
        cols = unit_start(core, zs)
        gate_side, up_side = unit_sides(core, zs)
        return mm(gate_side, wg[:, cols], 1, 1) + mm(up_side, wu[:, cols], 1, 1)

    def unit_grads(core, zs):
        cols = unit_start(core, zs)
        gate_side, up_side = unit_sides(core, zs)
        hid = [unpack_b(hid_blocks[z * 2 + core]) for z in zs]
        hid = jnp.concatenate(hid, axis=1).astype(BF16)
        gwd_ref[0, cols, :] = mm(hid, scaled, 0, 0).astype(BF16)
        gwg_ref[0, :, cols] = mm(x, gate_side, 0, 0).astype(BF16)
        gwu_ref[0, :, cols] = mm(x, up_side, 0, 0).astype(BF16)

    for k in range(nz - 1):
        ag_forward(0, k)
    if width % 128 == 0:
        back = unit_back(my_c, [my_z])
        unit_grads(my_c, [my_z])
        ag_finish(0, 0)
        ag_finish(1, 0)
        back = back + unit_back(other_c, [my_z])
        unit_grads(other_c, [my_z])
        late = []
        for k, peer in enumerate(chips):
            ag_forward(1, k)
            back = back + unit_back(my_c, [peer])
            if k + 1 < len(chips):
                unit_grads(my_c, [peer])
            else:
                late.append((my_c, [peer]))
        for k, peer in enumerate(chips):
            ag_finish(0, k + 1)
            ag_finish(1, k + 1)
            back = back + unit_back(other_c, [peer])
            late.append((other_c, [peer]))
    else:
        for k in range(nz - 1):
            ag_forward(1, k)
        back = unit_back(my_c, list(range(nz)))
        for k in range(nz):
            ag_finish(0, k)
            ag_finish(1, k)
        back = back + unit_back(other_c, list(range(nz)))
        late = [(my_c, list(range(nz))), (other_c, list(range(nz)))]
    back = back.astype(BF16)

    for k, peer in enumerate(d_peers):
        part_copy(k, peer, peer).wait_recv()
    gates_sum = sum(part_blocks[d] for d in range(nd))
    gate_lines = []
    for k in range(cfg.gate_rows):
        gate_lines += split_two(gates_sum[k : k + 1])
    lines = pad_rows(jnp.concatenate(gate_lines, axis=0), cfg.back_rows - rb)
    if width < fc:
        lines = jnp.concatenate([lines, jnp.zeros((lines.shape[0], fc - width), F32)], axis=1)
    for o in range(nx):
        mask = rank_mask(slot_row, o * tok, (o + 1) * tok, rb, 1).astype(F32).astype(BF16)
        back_send[o] = jnp.concatenate([mm(mask, back, 1, 0), lines], axis=0).astype(BF16)
    back_recv[me_x] = back_send[me_x]

    def back_copy(k, peer, slot):
        return remote(
            back_send.at[peer], back_recv.at[slot], back_ssem.at[k], back_rsem.at[slot], (me_d, peer)
        )

    for k, peer in enumerate(x_peers):
        launch(back_copy(k, peer, me_x))

    for core, zs in late:
        unit_grads(core, zs)
    for k, peer in enumerate(x_peers):
        back_copy(k, peer, peer).wait_recv()
    for e in range(flight):
        ret_ref[e] = sum(back_recv[e * GROUP + q, :rb].astype(F32) for q in range(GROUP))
    gsum_ref[...] = sum(
        back_recv[expert_here * GROUP + q, rb:].astype(F32)[:, :width] for q in range(GROUP)
    )
    for copy in sends:
        copy.wait_send()


def pieces(rows):
    step = rows // PIECES
    return [pl.ds(j * step, step) for j in range(PIECES)]


def finish_kernel(
    cfg,
    gwg_ref,
    gwu_ref,
    gwd_ref,
    ret_ref,
    gsum_ref,
    where_ref,
    tok_out,
    wg_out,
    wu_out,
    wd_out,
    gates_out,
    tok_vmem,
    sem,
):
    copies = [
        pltpu.make_async_copy(src.at[:, rows], dst.at[:, rows], sem.at[i, j])
        for i, (src, dst) in enumerate(((gwg_ref, wg_out), (gwu_ref, wu_out), (gwd_ref, wd_out)))
        for j, rows in enumerate(pieces(src.shape[1]))
    ]
    for copy in copies:
        copy.start()
    me_x = lax.axis_index("expert")
    total = None
    for e in range(cfg.flight):
        spread = (where_ref[e] == iota((cfg.rb, cfg.tok), 1)).astype(F32).astype(BF16)
        term = mm(spread, ret_ref[e].astype(BF16), 0, 0)
        total = term if total is None else total + term
    tok_vmem[...] = total.astype(BF16)
    copies.append(pltpu.make_async_copy(tok_vmem, tok_out, sem.at[3, 0]))
    copies[-1].start()
    wide = cfg.cap // GROUP
    first = lax.rem(me_x, GROUP) * wide
    gates = jnp.zeros((1, wide), F32)
    for k in range(cfg.gate_rows):
        line = gsum_ref[2 * k : 2 * k + 1, :] + gsum_ref[2 * k + 1 : 2 * k + 2, :]
        shape = (wide, cfg.width)
        here = iota(shape, 1) + k * cfg.width == iota(shape, 0) + first
        column = jnp.sum(jnp.where(here, line, 0.0), axis=1, keepdims=True)
        eye = iota((wide, wide), 0) == iota((wide, wide), 1)
        gates = gates + jnp.sum(jnp.where(eye, column, 0.0), axis=0, keepdims=True)
    gates_out[...] = gates
    for copy in copies:
        copy.wait()


class Sizes:
    pass


def per_device(mesh_shape, tokens, out_grad, slot_tokens, slot_gate, w_gate, w_up, w_down):
    c = Sizes()
    c.nx, nd = mesh_shape["expert"], mesh_shape["dp"]
    c.nz = nd // 2
    c.flight, c.cap = slot_tokens.shape
    c.tok, c.fc = tokens.shape
    ffq = w_gate.shape[2]
    c.half = ffq // 2
    c.width = c.half // c.nz
    most = 20
    c.rb = ceil_to(most, 8)
    c.gate_rows = ceil_to(c.cap, c.width) // c.width
    c.part_rows = ceil_to(c.gate_rows, 8)
    c.fold_b, c.fold_pick = c.width % 256 == 0, c.fc % 256 == 0
    c.rows_a = ceil_to(2 * c.cap, 16)
    c.rows_b, cols_b = (c.rows_a, c.width // 2) if c.fold_b else (ceil_to(c.cap, 16), c.width)
    pick = (ceil_to(2 * c.rb, 16), c.fc // 2) if c.fold_pick else (ceil_to(c.rb, 16), c.fc)
    c.back_rows = ceil_to(c.rb + 2 * c.gate_rows, 16)
    vmem = pl.BlockSpec(memory_space=pltpu.VMEM)
    hbm = pl.BlockSpec(memory_space=pltpu.HBM)
    dma = pltpu.SemaphoreType.DMA
    shape = jax.ShapeDtypeStruct
    grads = (
        shape((1, c.fc, ffq), BF16),
        shape((1, c.fc, ffq), BF16),
        shape((1, ffq, c.fc), BF16),
    )
    args = [
        pltpu.with_memory_space_constraint(value, pltpu.HBM)
        for value in (slot_tokens, slot_gate, tokens, out_grad, w_gate, w_up, w_down)
    ]
    parts = pl.pallas_call(
        functools.partial(exchange_kernel, c),
        out_shape=grads
        + (
            shape((c.flight, c.rb, c.fc), F32),
            shape((c.back_rows - c.rb, c.width), F32),
            shape((c.flight, c.rb, 1), jnp.int32),
        ),
        in_specs=[hbm] * 7,
        out_specs=[vmem] * 6,
        scratch_shapes=[
            pltpu.VMEM(slot_tokens.shape, jnp.int32),
            pltpu.VMEM(slot_gate.shape, F32),
            pltpu.VMEM((c.tok, c.fc), BF16),
            pltpu.VMEM((c.tok, c.fc), BF16),
            pltpu.VMEM((c.fc, ffq), BF16),
            pltpu.VMEM((c.fc, ffq), BF16),
            pltpu.VMEM((ffq, c.fc), BF16),
            pltpu.VMEM((c.flight, 2) + pick, BF16),
            pltpu.VMEM((c.nx, 2) + pick, BF16),
            pltpu.VMEM((2 * c.cap, c.half), F32),
            pltpu.VMEM((c.cap, c.half), F32),
            pltpu.VMEM((2 * c.cap, c.half), F32),
            pltpu.VMEM((c.cap, c.half), F32),
            pltpu.VMEM((c.nz, 2 * c.cap, c.width), F32),
            pltpu.VMEM((c.nz, c.cap, c.width), F32),
            pltpu.VMEM((c.nz, c.rows_a, c.width), BF16),
            pltpu.VMEM((c.nz, c.rows_b, cols_b), BF16),
            pltpu.VMEM((c.nz, c.rows_a, c.width), BF16),
            pltpu.VMEM((c.nz, c.rows_b, cols_b), BF16),
            pltpu.VMEM((nd, c.rows_b, cols_b), BF16),
            pltpu.VMEM((nd, c.rows_a, c.width), BF16),
            pltpu.VMEM((nd, c.part_rows, c.width), F32),
            pltpu.VMEM((c.nx, c.back_rows, c.fc), BF16),
            pltpu.VMEM((c.nx, c.back_rows, c.fc), BF16),
            dma((7,)),
            dma((2, c.nx)),
            dma((2, c.nx)),
            dma((2,)),
            dma((2,)),
            dma((2, c.nz)),
            dma((2, c.nz)),
            dma((2, c.nz, c.nz.bit_length())),
            dma((2, c.nz)),
            dma((2, nd)),
            dma((nd,)),
            dma((nd,)),
            dma((c.nx,)),
            dma((c.nx,)),
        ],
        compiler_params=pltpu.CompilerParams(
            collective_id=0, has_side_effects=True, vmem_limit_bytes=40 * 1024 * 1024
        ),
        name="exchange",
    )(*args)

    return pl.pallas_call(
        functools.partial(finish_kernel, c),
        out_shape=(shape((c.tok, c.fc), BF16),) + grads + (shape((1, c.cap // GROUP), F32),),
        in_specs=[vmem] * 6,
        out_specs=[hbm] * 4 + [vmem],
        scratch_shapes=[pltpu.VMEM((c.tok, c.fc), BF16), dma((4, PIECES))],
        compiler_params=pltpu.CompilerParams(vmem_limit_bytes=40 * 1024 * 1024),
        name="finish",
    )(*parts)


def solution(mesh):
    in_specs = (
        P("expert", "dp"),
        P("expert", "dp"),
        P(),
        P(),
        P("expert", "dp", None),
        P("expert", "dp", None),
        P("expert", None, "dp"),
    )
    out_specs = (
        P("expert", "dp"),
        P("expert", "dp", None),
        P("expert", "dp", None),
        P("expert", None, "dp"),
        P("expert", None),
    )
    return jax.shard_map(
        functools.partial(per_device, dict(mesh.shape)),
        mesh=mesh,
        in_specs=in_specs,
        out_specs=out_specs,
        check_vma=False,
    )
```
